32 devices in a mesh: section: 4 (over y, core), ctx: 8 (over z, x).
Axes of the slice: x: 2, y: 2, z: 4, core: 2. Of those that a mesh axis runs over, the one named last changes fastest.
Arguments:
- section_input: bfloat16 [2, 1024, 2048], P(None, 'ctx'), may hold values from -6 to 6
- cotangent: bfloat16 [2, 1024, 2048], P(None, 'ctx'), may hold values from -6 to 6
- w_query: bfloat16 [4, 2048, 1024], P('section', 'ctx'), may hold values from -0.125 to 0.125
- w_key: bfloat16 [4, 2048, 1024], P('section', 'ctx'), may hold values from -0.125 to 0.125
- w_value: bfloat16 [4, 2048, 1024], P('section', 'ctx'), may hold values from -0.125 to 0.125
- w_out: bfloat16 [4, 1024, 2048], P('section', 'ctx'), may hold values from -0.1875 to 0.1875
- block_mask: int32 [2, 32, 2], P(None, 'ctx'), may hold values 0 or 1
Outputs:
- section_output: bfloat16 [4, 2, 1024, 2048], P('section', None, 'ctx')
- input_grad: bfloat16 [4, 2, 1024, 2048], P('section', None, 'ctx')
The draws below stay inside these ranges and needn't reach their ends.
Inputs may be any that keep to these rules, and one draw needn't show every extreme that they name: A block always attends to itself; column 0 and 1 of block_mask choose its two neighbour blocks.
All inputs are finite; a program needn't handle non-finite values.
Results may differ from the reference program's by a relative error of at most 0.03.
Values may be sent and summed in bfloat16 or wider, within the bound.
A program may use at most 128 MiB of HBM per device.

```python
import jax
import jax.numpy as jnp
from jax import lax

D = 2048
HEADS = 8
HDIM = 128
MICRO = 2
BLK = 32
SEQ = 1024
NB = 32
SECTIONS = 4


def touch_ends(result, stream_key, low, largest):
    longest = result.shape.index(max(result.shape))
    spots = []
    for shift in (0, 1):
        where = [jax.random.randint(jax.random.fold_in(stream_key, axis), (), 0, length) for axis, length in enumerate(result.shape)]
        where[longest] = (where[longest] + shift) % result.shape[longest]
        spots.append(tuple(where))
    return result.at[spots[0]].set(low).at[spots[1]].set(largest)


def block_levels(own_key, dims, shards, least, high):
    def one(axis_at, blocks):
        heights = jax.random.uniform(jax.random.fold_in(jax.random.fold_in(own_key, 6), axis_at), (blocks,), jnp.float32, least / len(shards), high / len(shards))
        return jnp.repeat(jnp.exp(heights), dims[axis_at] // blocks).reshape((-1,) + (1,) * (len(dims) - axis_at - 1))

    factor_of = one(*shards[0])
    for cut in shards[1:]:
        factor_of = factor_of * one(*cut)
    return factor_of


def gaussian(stream_key, extent, deviation, limit, split=(), kind=jnp.bfloat16):
    entries = deviation * jax.random.normal(stream_key, extent, jnp.float32)
    if split:
        entries = entries * block_levels(stream_key, extent, split, -0.22, 0.18)
    return jnp.clip(entries, -limit, limit).astype(kind)


def setup_inputs(seed: int = 0) -> dict:
    arg_keys = jax.random.split(jax.random.key(seed), 8)
    section_input = gaussian(arg_keys[0], (MICRO, SEQ, D), 1.0, 6.0, ((1, 8),))
    cotangent = gaussian(arg_keys[1], (MICRO, SEQ, D), 1.0, 6.0, ((1, 8),))
    w_query = gaussian(arg_keys[2], (SECTIONS, D, HEADS * HDIM), D ** -0.5, 0.125, ((0, 4), (1, 8)))
    w_key = gaussian(arg_keys[3], (SECTIONS, D, HEADS * HDIM), D ** -0.5, 0.125, ((0, 4), (1, 8)))
    w_value = gaussian(arg_keys[4], (SECTIONS, D, HEADS * HDIM), D ** -0.5, 0.125, ((0, 4), (1, 8)))
    w_out = gaussian(arg_keys[5], (SECTIONS, HEADS * HDIM, D), (HEADS * HDIM) ** -0.5, 0.1875, ((0, 4), (1, 8)))
    block_mask = touch_ends((jax.random.randint(arg_keys[6], (MICRO, NB, 2), 0, 4) < 3).astype(jnp.int32), jax.random.fold_in(arg_keys[6], 1), 0, 1)
    return dict(section_input=section_input, cotangent=cotangent, w_query=w_query, w_key=w_key, w_value=w_value, w_out=w_out, block_mask=block_mask)


def rms_scale(values):
    return values * lax.rsqrt(lax.optimization_barrier(jnp.mean(values * values, axis=-1, keepdims=True)) + 1e-06)

def allowed_keys(mask_rows, block_ids, block_count):
    mask_float = mask_rows.astype(jnp.float32)
    left = mask_float[:, 0] * (block_ids > 0).astype(jnp.float32)
    right = mask_float[:, 1] * (block_ids < block_count - 1).astype(jnp.float32)
    return jnp.stack([left, jnp.ones_like(left), right], axis=1)

def project(layer_in, w_query, w_key, w_value):
    length = layer_in.shape[0]
    normed = rms_scale(layer_in.astype(jnp.float32)).astype(jnp.bfloat16)

    def head_normed(weight):
        out = jnp.dot(normed, weight, preferred_element_type=jnp.float32)
        out = rms_scale(out.reshape(length, HEADS, HDIM))
        return out.reshape(length, HEADS * HDIM).astype(jnp.bfloat16)
    query = head_normed(w_query)
    key = head_normed(w_key)
    value = jnp.dot(normed, w_value, preferred_element_type=jnp.float32).astype(jnp.bfloat16)
    return (query, key, value)

def attend(query, keys_ext, values_ext, allow, layer_in, w_out):
    length = query.shape[0]
    nblock = length // BLK
    queries = query.reshape(nblock, BLK, HEADS, HDIM)

    def windows(extended):
        grid = extended.reshape(nblock + 2, BLK, HEADS, HDIM)
        return jnp.concatenate([grid[:-2], grid[1:-1], grid[2:]], axis=1)
    keys = windows(keys_ext)
    values = windows(values_ext)
    scores = jnp.einsum('bqhd,bkhd->bhqk', queries, keys, preferred_element_type=jnp.float32) * HDIM ** (-0.5)
    weight = jnp.repeat(allow, BLK, axis=1)[:, None, None, :]
    probs = jnp.exp(scores) * weight
    total = lax.optimization_barrier(jnp.sum(probs, axis=-1))
    attended = jnp.einsum('bhqk,bkhd->bqhd', probs.astype(jnp.bfloat16), values, preferred_element_type=jnp.float32)
    attended = attended / jnp.transpose(total, (0, 2, 1))[..., None]
    attended = attended.reshape(length, HEADS * HDIM).astype(jnp.bfloat16)
    update = jnp.dot(attended, w_out, preferred_element_type=jnp.float32)
    return (layer_in.astype(jnp.float32) + update).astype(jnp.bfloat16)

def layer(layer_in, w_query, w_key, w_value, w_out, allow):
    query, key, value = project(layer_in, w_query, w_key, w_value)
    padding = jnp.zeros((BLK, HEADS * HDIM), jnp.bfloat16)
    keys_ext = jnp.concatenate([padding, key, padding], axis=0)
    values_ext = jnp.concatenate([padding, value, padding], axis=0)
    return attend(query, keys_ext, values_ext, allow, layer_in, w_out)

def reference(section_input, cotangent, w_query, w_key, w_value, w_out, block_mask):
    block_ids = jnp.arange(NB)
    outputs = []
    grads = []
    for micro_id in range(MICRO):
        allow = allowed_keys(block_mask[micro_id], block_ids, NB)
        current = section_input[micro_id]
        saved = []
        forward_out = []
        for section in range(SECTIONS):
            saved.append(current)
            current = layer(current, w_query[section], w_key[section], w_value[section], w_out[section], allow)
            forward_out.append(current)
        grad = cotangent[micro_id]
        backward_out = [None] * SECTIONS
        for section in reversed(range(SECTIONS)):

            def section_fn(values, section=section):
                return layer(values, w_query[section], w_key[section], w_value[section], w_out[section], allow)
            _, pull = jax.vjp(section_fn, saved[section])
            grad = pull(grad)[0]
            backward_out[section] = grad
        outputs.append(jnp.stack(forward_out))
        grads.append(jnp.stack(backward_out))
    return (jnp.stack(outputs, axis=1), jnp.stack(grads, axis=1))
```

```python
import functools

import jax
import jax.numpy as jnp
from jax import lax
from jax.experimental import pallas as pl
from jax.experimental.pallas import tpu as pltpu
from jax.sharding import PartitionSpec as P

D = 2048
HEADS = 8
HDIM = 128
WIDTH = HEADS * HDIM
BLK = 32
EPS = 1e-06
EXT = 256
STEP = 512
MESH = pl.DeviceIdType.MESH
F32 = jnp.float32
BF16 = jnp.bfloat16


def grid_of(n_ctx):
    wide = 1
    while (2 * wide) * (2 * wide) * 2 <= n_ctx:
        wide *= 2
    return n_ctx // wide, wide


def dot(a, b, dims=((1,), (0,))):
    return lax.dot_general(a, b, (dims, ((), ())), preferred_element_type=F32)


def head_mean(values):
    return jnp.mean(values, axis=-1, keepdims=True)


def kernel(
    n_section, n_ctx, micro, length,
    x0_ref, cot_ref, wq_in, wk_in, wv_in, wo_in, mask_ref,
    out_ref, grad_ref,
    wq, wk, wv, wo, xbuf, gbuf, nbuf, qbuf, rq, rk, kv, att, inv_total, probs,
    datt, dq, dkv, rims, dn,
    g_recv, g_send, own_sem, x_recv, x_send, b_recv, b_send, h_recv, h_send, r_recv, r_send, in_sem,
):
    section = lax.axis_index("section")
    place = lax.axis_index("ctx")
    tall, wide = grid_of(n_ctx)
    z = place // wide
    x = place % wide
    rows_all = micro * length

    around = (
        (z + 1 < tall, {"ctx": place + wide}),
        (z > 0, {"ctx": place - wide}),
        (x + 1 < wide, {"ctx": place + 1}),
        (x > 0, {"ctx": place - 1}),
    )
    has_right, right = place + 1 < n_ctx, {"ctx": place + 1}
    has_left, left = place > 0, {"ctx": place - 1}
    has_next, following = section + 1 < n_section, {"section": section + 1}
    has_prev, previous = section > 0, {"section": section - 1}

    barrier = pltpu.get_barrier_semaphore()
    friends = around + ((has_right, right), (has_left, left), (has_next, following), (has_prev, previous))
    count = 0
    for there, device in friends:
        @pl.when(there)
        def _(device=device):
            pl.semaphore_signal(barrier, inc=1, device_id=device, device_id_type=MESH)
        count = count + there.astype(jnp.int32)
    pl.semaphore_wait(barrier, count)

    weights = ((wk_in, wk, False), (wv_in, wv, False), (wq_in, wq, False), (wo_in, wo, True))

    def part(a, shard):
        rows = weights[a][0].shape[0]
        return weights[a][1].at[pl.ds(pl.multiple_of(shard * rows, rows), rows), :]

    def hop(a, shard, way, own):
        there, device = around[way]
        return there, pltpu.make_async_remote_copy(
            src_ref=weights[a][0] if own else part(a, shard),
            dst_ref=part(a, shard),
            send_sem=g_send.at[a, shard, way],
            recv_sem=g_recv.at[a, shard],
            device_id=device,
            device_id_type=MESH,
        )

    def ways_on(x_first, dz, dx):
        along_z = (0,) if dz > 0 else (1,)
        along_x = (2,) if dx > 0 else (3,)
        if x_first:
            return along_z if dz else along_x + (0, 1)
        return along_x if dx else along_z + (2, 3)

    offsets = [
        (dz, dx)
        for dz in range(1 - tall, tall)
        for dx in range(1 - wide, wide)
        if (dz, dx) != (0, 0)
    ]
    offsets.sort(key=lambda o: (abs(o[0]) + abs(o[1]), o))

    def gather(first):
        for a in range(4):
            for way in range(4):
                there, copy = hop(a, place, way, True)

                @pl.when(there)
                def _(copy=copy):
                    copy.start() if first else copy.wait_send()
        for dz, dx in offsets:
            zs, xs = z - dz, x - dx
            inside = (zs >= 0) & (zs < tall) & (xs >= 0) & (xs < wide)

            @pl.when(inside)
            def _(dz=dz, dx=dx, shard=zs * wide + xs):
                for a in range(4):
                    if first:
                        hop(a, shard, 0, False)[1].wait_recv()
                    for way in ways_on(weights[a][2], dz, dx):
                        there, copy = hop(a, shard, way, False)

                        @pl.when(there)
                        def _(copy=copy):
                            copy.start() if first else copy.wait_send()

    own_copies = [
        pltpu.make_async_copy(weights[a][0], part(a, place), own_sem.at[a]) for a in range(4)
    ]
    x_copy = pltpu.make_async_copy(x0_ref, xbuf, in_sem.at[0])
    g_copy = pltpu.make_async_copy(cot_ref, gbuf, in_sem.at[1])
    for copy in own_copies:
        copy.start()

    @pl.when(section == 0)
    def _():
        x_copy.start()

    @pl.when(section == n_section - 1)
    def _():
        g_copy.start()

    kv[...] = jnp.zeros_like(kv)
    rims[...] = jnp.zeros_like(rims)
    gather(True)
    for copy in own_copies:
        copy.wait()

    def relay(source, target, send, recv, device, c):
        cols = pl.ds(c * STEP, STEP)
        return pltpu.make_async_remote_copy(
            src_ref=source.at[:, cols], dst_ref=target.at[:, cols],
            send_sem=send.at[c], recv_sem=recv.at[c], device_id=device, device_id_type=MESH,
        )

    n_relay = D // STEP

    @pl.when(section == 0)
    def _():
        x_copy.wait()

    @pl.when(has_prev)
    def _():
        for c in range(n_relay):
            relay(out_ref, xbuf, x_send, x_recv, previous, c).wait_recv()

    chunk = 64

    @pl.loop(0, rows_all // chunk)
    def _(i):
        rows = pl.ds(pl.multiple_of(i * chunk, chunk), chunk)
        values = xbuf[rows, :].astype(F32)
        nbuf[rows, :] = (values * lax.rsqrt(head_mean(values * values) + EPS)).astype(BF16)

    def norm_heads(values):
        scales = []
        for h in range(STEP // HDIM):
            one = values[:, h * HDIM:(h + 1) * HDIM]
            scale = lax.rsqrt(head_mean(one * one) + EPS)
            scales.append(jnp.broadcast_to(scale, one.shape))
        return jnp.concatenate(scales, axis=1)

    @pl.loop(0, WIDTH // STEP)
    def _(i):
        cols = pl.ds(pl.multiple_of(i * STEP, STEP), STEP)
        out = dot(nbuf[...], wk[:, cols])
        scale = norm_heads(out)
        rk[:, cols] = scale
        key = (out * scale).astype(BF16)
        for m in range(micro):
            kv[0, m, BLK:BLK + length, cols] = key[m * length:(m + 1) * length]
        value = dot(nbuf[...], wv[:, cols]).astype(BF16)
        for m in range(micro):
            kv[1, m, BLK:BLK + length, cols] = value[m * length:(m + 1) * length]

    def to_right():
        return pltpu.make_async_remote_copy(
            src_ref=kv.at[:, :, pl.ds(length, BLK), :], dst_ref=kv.at[:, :, pl.ds(0, BLK), :],
            send_sem=h_send.at[0], recv_sem=h_recv.at[0], device_id=right, device_id_type=MESH,
        )

    def to_left():
        return pltpu.make_async_remote_copy(
            src_ref=kv.at[:, :, pl.ds(BLK, BLK), :], dst_ref=kv.at[:, :, pl.ds(BLK + length, BLK), :],
            send_sem=h_send.at[1], recv_sem=h_recv.at[1], device_id=left, device_id_type=MESH,
        )

    @pl.when(has_right)
    def _():
        to_right().start()

    @pl.when(has_left)
    def _():
        to_left().start()

    @pl.loop(0, WIDTH // STEP)
    def _(i):
        cols = pl.ds(pl.multiple_of(i * STEP, STEP), STEP)
        out = dot(nbuf[...], wq[:, cols])
        scale = norm_heads(out)
        rq[:, cols] = scale
        qbuf[:, cols] = (out * scale).astype(BF16)

    @pl.when(has_left)
    def _():
        to_right().wait_recv()

    @pl.when(has_right)
    def _():
        to_left().wait_recv()

    @pl.loop(0, HEADS)
    def _(h):
        cols = pl.ds(pl.multiple_of(h * HDIM, HDIM), HDIM)
        for m in range(micro):
            rows = slice(m * length, (m + 1) * length)
            scores = dot(qbuf[rows, cols], kv[0, m, :, cols], ((1,), (1,))) * HDIM ** (-0.5)
            prob = jnp.exp(scores) * mask_ref[m]
            probs[m, h] = prob
            inv = 1.0 / jnp.sum(prob, axis=-1, keepdims=True)
            inv_total[rows, cols] = jnp.broadcast_to(inv, (length, HDIM))
            att[rows, cols] = (dot(prob.astype(BF16), kv[1, m, :, cols]) * inv).astype(BF16)

    for c in range(n_relay):
        cols = slice(c * STEP, (c + 1) * STEP)
        update = dot(att[...], wo[:, cols])
        out_ref[:, cols] = (xbuf[:, cols].astype(F32) + update).astype(BF16)

        @pl.when(has_next)
        def _(c=c):
            relay(out_ref, xbuf, x_send, x_recv, following, c).start()

    @pl.when(section == n_section - 1)
    def _():
        g_copy.wait()

    @pl.when(has_next)
    def _():
        for c in range(n_relay):
            relay(grad_ref, gbuf, b_send, b_recv, following, c).wait_recv()

    @pl.loop(0, WIDTH // STEP)
    def _(i):
        cols = pl.ds(pl.multiple_of(i * STEP, STEP), STEP)
        datt[:, cols] = dot(gbuf[...], wo[cols, :], ((1,), (1,))).astype(BF16)

    @pl.loop(0, HEADS)
    def _(h):
        cols = pl.ds(pl.multiple_of(h * HDIM, HDIM), HDIM)
        for m in range(micro):
            rows = slice(m * length, (m + 1) * length)
            prob = probs[m, h]
            d_att = datt[rows, cols].astype(F32)
            inv = inv_total[rows, cols]
            d_sum = (d_att * inv)
            d_total = jnp.sum(d_sum * att[rows, cols].astype(F32), axis=-1, keepdims=True)
            d_sum = d_sum.astype(BF16)
            d_prob = dot(d_sum, kv[1, m, :, cols], ((1,), (1,))) - d_total
            d_score = (d_prob * prob * HDIM ** (-0.5)).astype(BF16)
            dkv[1, m, :, cols] = dot(prob.astype(BF16), d_sum, ((0,), (0,))).astype(BF16)
            dkv[0, m, :, cols] = dot(d_score, qbuf[rows, cols], ((0,), (0,))).astype(BF16)
            d_query = dot(d_score, kv[0, m, :, cols])
            query = qbuf[rows, cols].astype(F32)
            d_query = (d_query - query * head_mean(d_query * query)) * rq[rows, cols]
            dq[rows, cols] = d_query.astype(BF16)

    def rim_left():
        return pltpu.make_async_remote_copy(
            src_ref=dkv.at[:, :, pl.ds(0, BLK), :], dst_ref=rims.at[1],
            send_sem=r_send.at[0], recv_sem=r_recv.at[0], device_id=left, device_id_type=MESH,
        )

    def rim_right():
        return pltpu.make_async_remote_copy(
            src_ref=dkv.at[:, :, pl.ds(BLK + length, BLK), :], dst_ref=rims.at[0],
            send_sem=r_send.at[1], recv_sem=r_recv.at[1], device_id=right, device_id_type=MESH,
        )

    @pl.when(has_left)
    def _():
        rim_left().start()

    @pl.when(has_right)
    def _():
        rim_right().start()

    @pl.loop(0, D // STEP)
    def _(i):
        cols = pl.ds(pl.multiple_of(i * STEP, STEP), STEP)
        dn[:, cols] = dot(dq[...], wq[cols, :], ((1,), (1,)))

    @pl.when(has_right)
    def _():
        rim_left().wait_recv()

    @pl.when(has_left)
    def _():
        rim_right().wait_recv()

    for which in range(2):
        for m in range(micro):
            for side, start in ((0, BLK), (1, length)):
                rows = slice(start, start + BLK)
                dkv[which, m, rows] = dkv[which, m, rows] + rims[side, which, m]

    @pl.loop(0, HEADS)
    def _(h):
        cols = pl.ds(pl.multiple_of(h * HDIM, HDIM), HDIM)
        for m in range(micro):
            rows = slice(m * length, (m + 1) * length)
            d_key = dkv[0, m, BLK:BLK + length, cols].astype(F32)
            key = kv[0, m, BLK:BLK + length, cols].astype(F32)
            d_key = (d_key - key * head_mean(d_key * key)) * rk[rows, cols]
            dq[rows, cols] = d_key.astype(BF16)
            datt[rows, cols] = dkv[1, m, BLK:BLK + length, cols]

    @pl.loop(0, D // STEP)
    def _(i):
        cols = pl.ds(pl.multiple_of(i * STEP, STEP), STEP)
        dn[:, cols] = (
            dn[:, cols]
            + dot(dq[...], wk[cols, :], ((1,), (1,)))
            + dot(datt[...], wv[cols, :], ((1,), (1,)))
        )

    @pl.loop(0, rows_all // chunk)
    def _(i):
        rows = pl.ds(pl.multiple_of(i * chunk, chunk), chunk)
        values = xbuf[rows, :].astype(F32)
        scale = lax.rsqrt(head_mean(values * values) + EPS)
        d_norm = dn[rows, :].astype(BF16).astype(F32)
        normed = values * scale
        d_in = scale * (d_norm - normed * head_mean(d_norm * normed))
        grad_ref[rows, :] = (gbuf[rows, :].astype(F32) + d_in.astype(BF16).astype(F32)).astype(BF16)

    @pl.when(has_prev)
    def _():
        for c in range(n_relay):
            relay(grad_ref, gbuf, b_send, b_recv, previous, c).start()

    gather(False)

    @pl.when(has_next)
    def _():
        for c in range(n_relay):
            relay(out_ref, xbuf, x_send, x_recv, following, c).wait_send()

    @pl.when(has_right)
    def _():
        to_right().wait_send()
        rim_right().wait_send()

    @pl.when(has_left)
    def _():
        to_left().wait_send()
        rim_left().wait_send()

    @pl.when(has_prev)
    def _():
        for c in range(n_relay):
            relay(grad_ref, gbuf, b_send, b_recv, previous, c).wait_send()


def mask_weights(block_mask, place, n_ctx, length):
    blocks = length // BLK
    ids = place * blocks + jnp.arange(blocks)
    mask = block_mask.astype(F32)
    before = mask[:, :, 0] * (ids > 0).astype(F32)
    after = mask[:, :, 1] * (ids < blocks * n_ctx - 1).astype(F32)
    offset = jnp.arange(EXT)[None, :] // BLK - jnp.arange(length)[:, None] // BLK
    def rows(values):
        return jnp.repeat(values, BLK, axis=1)[:, :, None]
    return jnp.where(offset == 0, rows(before), jnp.where(offset == 1, 1.0, jnp.where(offset == 2, rows(after), 0.0)))


def per_device(n_section, n_ctx, section_input, cotangent, w_query, w_key, w_value, w_out, block_mask):
    micro, length = section_input.shape[:2]
    rows = micro * length
    mask = mask_weights(block_mask, lax.axis_index("ctx"), n_ctx, length)
    any_space = pl.BlockSpec(memory_space=pl.ANY)
    vmem = pl.BlockSpec(memory_space=pltpu.VMEM)
    dma = pltpu.SemaphoreType.DMA
    n_relay = D // STEP
    out, grad = pl.pallas_call(
        functools.partial(kernel, n_section, n_ctx, micro, length),
        out_shape=[jax.ShapeDtypeStruct((rows, D), BF16)] * 2,
        in_specs=[any_space] * 6 + [vmem],
        out_specs=[vmem, vmem],
        scratch_shapes=[
            pltpu.VMEM((D, WIDTH), BF16),
            pltpu.VMEM((D, WIDTH), BF16),
            pltpu.VMEM((D, WIDTH), BF16),
            pltpu.VMEM((WIDTH, D), BF16),
            pltpu.VMEM((rows, D), BF16),
            pltpu.VMEM((rows, D), BF16),
            pltpu.VMEM((rows, D), BF16),
            pltpu.VMEM((rows, WIDTH), BF16),
            pltpu.VMEM((rows, WIDTH), F32),
            pltpu.VMEM((rows, WIDTH), F32),
            pltpu.VMEM((2, micro, EXT, WIDTH), BF16),
            pltpu.VMEM((rows, WIDTH), BF16),
            pltpu.VMEM((rows, WIDTH), F32),
            pltpu.VMEM((micro, HEADS, length, EXT), F32),
            pltpu.VMEM((rows, WIDTH), BF16),
            pltpu.VMEM((rows, WIDTH), BF16),
            pltpu.VMEM((2, micro, EXT, WIDTH), BF16),
            pltpu.VMEM((2, 2, micro, BLK, WIDTH), BF16),
            pltpu.VMEM((rows, D), F32),
            dma((4, n_ctx)),
            dma((4, n_ctx, 4)),
            dma((4,)),
            dma((n_relay,)),
            dma((n_relay,)),
            dma((n_relay,)),
            dma((n_relay,)),
            dma((2,)),
            dma((2,)),
            dma((2,)),
            dma((2,)),
            dma((2,)),
        ],
        compiler_params=pltpu.CompilerParams(
            collective_id=0, has_side_effects=True, vmem_limit_bytes=56 * 2**20
        ),
    )(
        section_input.reshape(rows, D), cotangent.reshape(rows, D),
        w_query[0], w_key[0], w_value[0], w_out[0], mask,
    )
    return out.reshape(1, micro, length, D), grad.reshape(1, micro, length, D)


def solution(mesh):
    return jax.shard_map(
        functools.partial(per_device, mesh.shape["section"], mesh.shape["ctx"]),
        mesh=mesh,
        in_specs=(
            P(None, "ctx", None),
            P(None, "ctx", None),
            P("section", "ctx", None),
            P("section", "ctx", None),
            P("section", "ctx", None),
            P("section", "ctx", None),
            P(None, "ctx", None),
        ),
        out_specs=(P("section", None, "ctx", None), P("section", None, "ctx", None)),
        check_vma=False,
    )
```

```python
import functools

import jax
import jax.numpy as jnp
from jax import lax
from jax.experimental import pallas as pl
from jax.experimental.pallas import tpu as pltpu
from jax.sharding import PartitionSpec as P

D = 2048
HEADS = 8
HDIM = 128
WIDTH = HEADS * HDIM
BLK = 32
EPS = 1e-06
EXT = 256
STEP = 512
MESH = pl.DeviceIdType.MESH
F32 = jnp.float32
BF16 = jnp.bfloat16


def grid_of(n_ctx):
    wide = 1
    while (2 * wide) * (2 * wide) * 2 <= n_ctx:
        wide *= 2
    return n_ctx // wide, wide


def dot(a, b, dims=((1,), (0,))):
    return lax.dot_general(a, b, (dims, ((), ())), preferred_element_type=F32)


def head_mean(values):
    return jnp.mean(values, axis=-1, keepdims=True)


def kernel(
    n_section, n_ctx, micro, length,
    x0_ref, cot_ref, wq_in, wk_in, wv_in, wo_in, mask_ref,
    out_ref, grad_ref,
    wq, wk, wv, wo, xbuf, gbuf, nbuf, qbuf, rq, rk, kv, att, inv_total, probs,
    datt, dq, dkv, rims, dn,
    g_recv, g_send, own_sem, x_recv, x_send, b_recv, b_send, h_recv, h_send, r_recv, r_send, in_sem,
):
    section = lax.axis_index("section")
    place = lax.axis_index("ctx")
    tall, wide = grid_of(n_ctx)
    z = place // wide
    x = place % wide
    rows_all = micro * length

    around = (
        (z + 1 < tall, {"ctx": place + wide}),
        (z > 0, {"ctx": place - wide}),
        (x + 1 < wide, {"ctx": place + 1}),
        (x > 0, {"ctx": place - 1}),
    )
    has_right, right = place + 1 < n_ctx, {"ctx": place + 1}
    has_left, left = place > 0, {"ctx": place - 1}
    has_next, following = section + 1 < n_section, {"section": section + 1}
    has_prev, previous = section > 0, {"section": section - 1}

    barrier = pltpu.get_barrier_semaphore()
    friends = around + ((has_right, right), (has_left, left), (has_next, following), (has_prev, previous))
    count = 0
    for there, device in friends:
        @pl.when(there)
        def _(device=device):
            pl.semaphore_signal(barrier, inc=1, device_id=device, device_id_type=MESH)
        count = count + there.astype(jnp.int32)
    pl.semaphore_wait(barrier, count)

    deep, half = wk_in.shape[0], wo_in.shape[0] // 2
    weights = (
        (wk_in, wk, False, 0, deep), (wv_in, wv, False, 0, deep), (wq_in, wq, False, 0, deep),
        (wo_in, wo, True, 0, half), (wo_in, wo, False, half, half),
    )
    n_part = len(weights)

    def part(a, shard):
        source, whole, _, first, rows = weights[a]
        start = shard * source.shape[0] + first
        return whole.at[pl.ds(pl.multiple_of(start, rows), rows), :]

    def shard_of(a):
        return weights[a][0].at[pl.ds(weights[a][3], weights[a][4]), :]

    def hop(a, shard, way, own):
        there, device = around[way]
        return there, pltpu.make_async_remote_copy(
            src_ref=shard_of(a) if own else part(a, shard),
            dst_ref=part(a, shard),
            send_sem=g_send.at[a, shard, way],
            recv_sem=g_recv.at[a, shard],
            device_id=device,
            device_id_type=MESH,
        )

    def ways_on(x_first, dz, dx):
        along_z = (0,) if dz > 0 else (1,)
        along_x = (2,) if dx > 0 else (3,)
        if x_first:
            return along_z if dz else along_x + (0, 1)
        return along_x if dx else along_z + (2, 3)

    offsets = [
        (dz, dx)
        for dz in range(1 - tall, tall)
        for dx in range(1 - wide, wide)
        if (dz, dx) != (0, 0)
    ]
    offsets.sort(key=lambda o: (abs(o[0]) + abs(o[1]), o))

    def gather(first):
        for a in range(n_part):
            for way in range(4):
                there, copy = hop(a, place, way, True)

                @pl.when(there)
                def _(copy=copy):
                    copy.start() if first else copy.wait_send()
        for dz, dx in offsets:
            zs, xs = z - dz, x - dx
            inside = (zs >= 0) & (zs < tall) & (xs >= 0) & (xs < wide)

            @pl.when(inside)
            def _(dz=dz, dx=dx, shard=zs * wide + xs):
                for a in range(n_part):
                    if first:
                        hop(a, shard, 0, False)[1].wait_recv()
                    for way in ways_on(weights[a][2], dz, dx):
                        there, copy = hop(a, shard, way, False)

                        @pl.when(there)
                        def _(copy=copy):
                            copy.start() if first else copy.wait_send()

    own_copies = [
        pltpu.make_async_copy(shard_of(a), part(a, place), own_sem.at[a]) for a in range(n_part)
    ]
    x_copy = pltpu.make_async_copy(x0_ref, xbuf, in_sem.at[0])
    g_copy = pltpu.make_async_copy(cot_ref, gbuf, in_sem.at[1])
    for copy in own_copies:
        copy.start()

    @pl.when(section == 0)
    def _():
        x_copy.start()

    @pl.when(section == n_section - 1)
    def _():
        g_copy.start()

    kv[...] = jnp.zeros_like(kv)
    rims[...] = jnp.zeros_like(rims)
    gather(True)
    for copy in own_copies:
        copy.wait()

    def relay(source, target, send, recv, device, c):
        cols = pl.ds(c * STEP, STEP)
        return pltpu.make_async_remote_copy(
            src_ref=source.at[:, cols], dst_ref=target.at[:, cols],
            send_sem=send.at[c], recv_sem=recv.at[c], device_id=device, device_id_type=MESH,
        )

    n_relay = D // STEP
    chunk = 64
    n_back = rows_all // chunk

    def relay_back(device, i):
        rows = pl.ds(pl.multiple_of(i * chunk, chunk), chunk)
        return pltpu.make_async_remote_copy(
            src_ref=grad_ref.at[rows, :], dst_ref=gbuf.at[rows, :],
            send_sem=b_send.at[i], recv_sem=b_recv.at[i], device_id=device, device_id_type=MESH,
        )

    @pl.when(section == 0)
    def _():
        x_copy.wait()

    @pl.when(has_prev)
    def _():
        gather(False)
        for c in range(n_relay):
            relay(out_ref, xbuf, x_send, x_recv, previous, c).wait_recv()

    @pl.loop(0, rows_all // chunk)
    def _(i):
        rows = pl.ds(pl.multiple_of(i * chunk, chunk), chunk)
        values = xbuf[rows, :].astype(F32)
        nbuf[rows, :] = (values * lax.rsqrt(head_mean(values * values) + EPS)).astype(BF16)

    def norm_heads(values):
        scales = []
        for h in range(STEP // HDIM):
            one = values[:, h * HDIM:(h + 1) * HDIM]
            scale = lax.rsqrt(head_mean(one * one) + EPS)
            scales.append(jnp.broadcast_to(scale, one.shape))
        return jnp.concatenate(scales, axis=1)

    @pl.loop(0, WIDTH // STEP)
    def _(i):
        cols = pl.ds(pl.multiple_of(i * STEP, STEP), STEP)
        out = dot(nbuf[...], wk[:, cols])
        scale = norm_heads(out)
        rk[:, cols] = scale
        key = (out * scale).astype(BF16)
        for m in range(micro):
            kv[0, m, BLK:BLK + length, cols] = key[m * length:(m + 1) * length]
        value = dot(nbuf[...], wv[:, cols]).astype(BF16)
        for m in range(micro):
            kv[1, m, BLK:BLK + length, cols] = value[m * length:(m + 1) * length]

    def to_right():
        return pltpu.make_async_remote_copy(
            src_ref=kv.at[:, :, pl.ds(length, BLK), :], dst_ref=kv.at[:, :, pl.ds(0, BLK), :],
            send_sem=h_send.at[0], recv_sem=h_recv.at[0], device_id=right, device_id_type=MESH,
        )

    def to_left():
        return pltpu.make_async_remote_copy(
            src_ref=kv.at[:, :, pl.ds(BLK, BLK), :], dst_ref=kv.at[:, :, pl.ds(BLK + length, BLK), :],
            send_sem=h_send.at[1], recv_sem=h_recv.at[1], device_id=left, device_id_type=MESH,
        )

    @pl.when(has_right)
    def _():
        to_right().start()

    @pl.when(has_left)
    def _():
        to_left().start()

    @pl.loop(0, WIDTH // STEP)
    def _(i):
        cols = pl.ds(pl.multiple_of(i * STEP, STEP), STEP)
        out = dot(nbuf[...], wq[:, cols])
        scale = norm_heads(out)
        rq[:, cols] = scale
        qbuf[:, cols] = (out * scale).astype(BF16)

    @pl.when(has_left)
    def _():
        to_right().wait_recv()

    @pl.when(has_right)
    def _():
        to_left().wait_recv()

    @pl.loop(0, HEADS, unroll=4)
    def _(h):
        cols = pl.ds(pl.multiple_of(h * HDIM, HDIM), HDIM)
        for m in range(micro):
            rows = slice(m * length, (m + 1) * length)
            scores = dot(qbuf[rows, cols], kv[0, m, :, cols], ((1,), (1,))) * HDIM ** (-0.5)
            prob = jnp.exp(scores) * mask_ref[m]
            probs[m, h] = prob
            inv = 1.0 / jnp.sum(prob, axis=-1, keepdims=True)
            inv_total[rows, cols] = jnp.broadcast_to(inv, (length, HDIM))
            att[rows, cols] = (dot(prob.astype(BF16), kv[1, m, :, cols]) * inv).astype(BF16)

    for c in range(n_relay):
        cols = slice(c * STEP, (c + 1) * STEP)
        update = dot(att[...], wo[:, cols])
        out_ref[:, cols] = (xbuf[:, cols].astype(F32) + update).astype(BF16)

        @pl.when(has_next)
        def _(c=c):
            relay(out_ref, xbuf, x_send, x_recv, following, c).start()

    @pl.when(section == 0)
    def _():
        gather(False)

    @pl.when(has_next)
    def _():
        for c in range(n_relay):
            relay(out_ref, xbuf, x_send, x_recv, following, c).wait_send()

    @pl.when(section == n_section - 1)
    def _():
        g_copy.wait()

    for m in range(micro):
        rows = slice(m * length, (m + 1) * length)

        @pl.when(has_next)
        def _(m=m):
            for i in range(m * length // chunk, (m + 1) * length // chunk):
                relay_back(following, i).wait_recv()

        @pl.loop(0, WIDTH // STEP)
        def _(i, rows=rows):
            cols = pl.ds(pl.multiple_of(i * STEP, STEP), STEP)
            datt[rows, cols] = dot(gbuf[rows, :], wo[cols, :], ((1,), (1,))).astype(BF16)

        @pl.loop(0, HEADS, unroll=4)
        def _(h, m=m, rows=rows):
            cols = pl.ds(pl.multiple_of(h * HDIM, HDIM), HDIM)
            prob = probs[m, h]
            d_att = datt[rows, cols].astype(F32)
            d_sum = d_att * inv_total[rows, cols]
            d_total = jnp.sum(d_sum * att[rows, cols].astype(F32), axis=-1, keepdims=True)
            d_sum = d_sum.astype(BF16)
            d_prob = dot(d_sum, kv[1, m, :, cols], ((1,), (1,))) - d_total
            d_score = (d_prob * prob * HDIM ** (-0.5)).astype(BF16)
            dkv[1, m, :, cols] = dot(prob.astype(BF16), d_sum, ((0,), (0,))).astype(BF16)
            dkv[0, m, :, cols] = dot(d_score, qbuf[rows, cols], ((0,), (0,))).astype(BF16)
            d_query = dot(d_score, kv[0, m, :, cols])
            query = qbuf[rows, cols].astype(F32)
            d_query = (d_query - query * head_mean(d_query * query)) * rq[rows, cols]
            dq[rows, cols] = d_query.astype(BF16)

    def rim_left():
        return pltpu.make_async_remote_copy(
            src_ref=dkv.at[:, :, pl.ds(0, BLK), :], dst_ref=rims.at[1],
            send_sem=r_send.at[0], recv_sem=r_recv.at[0], device_id=left, device_id_type=MESH,
        )

    def rim_right():
        return pltpu.make_async_remote_copy(
            src_ref=dkv.at[:, :, pl.ds(BLK + length, BLK), :], dst_ref=rims.at[0],
            send_sem=r_send.at[1], recv_sem=r_recv.at[1], device_id=right, device_id_type=MESH,
        )

    @pl.when(has_left)
    def _():
        rim_left().start()

    @pl.when(has_right)
    def _():
        rim_right().start()

    @pl.loop(0, D // STEP)
    def _(i):
        cols = pl.ds(pl.multiple_of(i * STEP, STEP), STEP)
        dn[:, cols] = dot(dq[...], wq[cols, :], ((1,), (1,)))

    @pl.when(has_right)
    def _():
        rim_left().wait_recv()

    @pl.when(has_left)
    def _():
        rim_right().wait_recv()

    for which in range(2):
        for m in range(micro):
            for side, start in ((0, BLK), (1, length)):
                rows = slice(start, start + BLK)
                dkv[which, m, rows] = dkv[which, m, rows] + rims[side, which, m]

    @pl.loop(0, HEADS, unroll=4)
    def _(h):
        cols = pl.ds(pl.multiple_of(h * HDIM, HDIM), HDIM)
        for m in range(micro):
            rows = slice(m * length, (m + 1) * length)
            d_key = dkv[0, m, BLK:BLK + length, cols].astype(F32)
            key = kv[0, m, BLK:BLK + length, cols].astype(F32)
            d_key = (d_key - key * head_mean(d_key * key)) * rk[rows, cols]
            dq[rows, cols] = d_key.astype(BF16)
            datt[rows, cols] = dkv[1, m, BLK:BLK + length, cols]

    @pl.loop(0, D // STEP)
    def _(i):
        cols = pl.ds(pl.multiple_of(i * STEP, STEP), STEP)
        dn[:, cols] = (
            dn[:, cols]
            + dot(dq[...], wk[cols, :], ((1,), (1,)))
            + dot(datt[...], wv[cols, :], ((1,), (1,)))
        )

    @pl.loop(0, rows_all // chunk)
    def _(i):
        rows = pl.ds(pl.multiple_of(i * chunk, chunk), chunk)
        values = xbuf[rows, :].astype(F32)
        scale = lax.rsqrt(head_mean(values * values) + EPS)
        d_norm = dn[rows, :].astype(BF16).astype(F32)
        normed = values * scale
        d_in = scale * (d_norm - normed * head_mean(d_norm * normed))
        grad_ref[rows, :] = (gbuf[rows, :].astype(F32) + d_in.astype(BF16).astype(F32)).astype(BF16)

        @pl.when(has_prev)
        def _():
            relay_back(previous, i).start()

    @pl.when(has_right)
    def _():
        to_right().wait_send()
        rim_right().wait_send()

    @pl.when(has_left)
    def _():
        to_left().wait_send()
        rim_left().wait_send()

    @pl.when(has_prev)
    def _():
        for i in range(n_back):
            relay_back(previous, i).wait_send()


def mask_weights(block_mask, place, n_ctx, length):
    blocks = length // BLK
    ids = place * blocks + jnp.arange(blocks)
    mask = block_mask.astype(F32)
    before = mask[:, :, 0] * (ids > 0).astype(F32)
    after = mask[:, :, 1] * (ids < blocks * n_ctx - 1).astype(F32)
    offset = jnp.arange(EXT)[None, :] // BLK - jnp.arange(length)[:, None] // BLK
    def rows(values):
        return jnp.repeat(values, BLK, axis=1)[:, :, None]
    return jnp.where(offset == 0, rows(before), jnp.where(offset == 1, 1.0, jnp.where(offset == 2, rows(after), 0.0)))


def per_device(n_section, n_ctx, section_input, cotangent, w_query, w_key, w_value, w_out, block_mask):
    micro, length = section_input.shape[:2]
    rows = micro * length
    mask = mask_weights(block_mask, lax.axis_index("ctx"), n_ctx, length)
    any_space = pl.BlockSpec(memory_space=pl.ANY)
    vmem = pl.BlockSpec(memory_space=pltpu.VMEM)
    dma = pltpu.SemaphoreType.DMA
    n_relay = D // STEP
    out, grad = pl.pallas_call(
        functools.partial(kernel, n_section, n_ctx, micro, length),
        out_shape=[jax.ShapeDtypeStruct((rows, D), BF16)] * 2,
        in_specs=[any_space] * 6 + [vmem],
        out_specs=[vmem, vmem],
        scratch_shapes=[
            pltpu.VMEM((D, WIDTH), BF16),
            pltpu.VMEM((D, WIDTH), BF16),
            pltpu.VMEM((D, WIDTH), BF16),
            pltpu.VMEM((WIDTH, D), BF16),
            pltpu.VMEM((rows, D), BF16),
            pltpu.VMEM((rows, D), BF16),
            pltpu.VMEM((rows, D), BF16),
            pltpu.VMEM((rows, WIDTH), BF16),
            pltpu.VMEM((rows, WIDTH), F32),
            pltpu.VMEM((rows, WIDTH), F32),
            pltpu.VMEM((2, micro, EXT, WIDTH), BF16),
            pltpu.VMEM((rows, WIDTH), BF16),
            pltpu.VMEM((rows, WIDTH), F32),
            pltpu.VMEM((micro, HEADS, length, EXT), F32),
            pltpu.VMEM((rows, WIDTH), BF16),
            pltpu.VMEM((rows, WIDTH), BF16),
            pltpu.VMEM((2, micro, EXT, WIDTH), BF16),
            pltpu.VMEM((2, 2, micro, BLK, WIDTH), BF16),
            pltpu.VMEM((rows, D), F32),
            dma((5, n_ctx)),
            dma((5, n_ctx, 4)),
            dma((5,)),
            dma((n_relay,)),
            dma((n_relay,)),
            dma((rows // 64,)),
            dma((rows // 64,)),
            dma((2,)),
            dma((2,)),
            dma((2,)),
            dma((2,)),
            dma((2,)),
        ],
        compiler_params=pltpu.CompilerParams(
            collective_id=0, has_side_effects=True, vmem_limit_bytes=56 * 2**20
        ),
    )(
        section_input.reshape(rows, D), cotangent.reshape(rows, D),
        w_query[0], w_key[0], w_value[0], w_out[0], mask,
    )
    return out.reshape(1, micro, length, D), grad.reshape(1, micro, length, D)


def solution(mesh):
    return jax.shard_map(
        functools.partial(per_device, mesh.shape["section"], mesh.shape["ctx"]),
        mesh=mesh,
        in_specs=(
            P(None, "ctx", None),
            P(None, "ctx", None),
            P("section", "ctx", None),
            P("section", "ctx", None),
            P("section", "ctx", None),
            P("section", "ctx", None),
            P(None, "ctx", None),
        ),
        out_specs=(P("section", None, "ctx", None), P("section", None, "ctx", None)),
        check_vma=False,
    )
```

```python
import functools

import jax
import jax.numpy as jnp
from jax import lax
from jax.experimental import pallas as pl
from jax.experimental.pallas import tpu as pltpu
from jax.sharding import PartitionSpec as P

D = 2048
HEADS = 8
HDIM = 128
WIDTH = HEADS * HDIM
BLK = 32
EPS = 1e-06
EXT = 256
STEP = 512
MESH = pl.DeviceIdType.MESH
F32 = jnp.float32
BF16 = jnp.bfloat16


def grid_of(n_ctx):
    wide = 1
    while (2 * wide) * (2 * wide) * 2 <= n_ctx:
        wide *= 2
    return n_ctx // wide, wide


def dot(a, b, dims=((1,), (0,))):
    return lax.dot_general(a, b, (dims, ((), ())), preferred_element_type=F32)


def head_mean(values):
    return jnp.mean(values, axis=-1, keepdims=True)


def kernel(
    n_section, n_ctx, micro, length,
    x0_ref, cot_ref, wq_in, wk_in, wv_in, wo_in, mask_ref,
    out_ref, grad_ref,
    wq, wk, wv, wo, xbuf, gbuf, nbuf, qbuf, rq, rk, kv, att, inv_total, probs,
    datt, dq, dkv, rims, dn,
    g_recv, g_send, own_sem, x_recv, x_send, b_recv, b_send, h_recv, h_send, r_recv, r_send, in_sem, go_sem,
):
    section = lax.axis_index("section")
    place = lax.axis_index("ctx")
    tall, wide = grid_of(n_ctx)
    z = place // wide
    x = place % wide
    rows_all = micro * length

    around = (
        (z + 1 < tall, {"ctx": place + wide}),
        (z > 0, {"ctx": place - wide}),
        (x + 1 < wide, {"ctx": place + 1}),
        (x > 0, {"ctx": place - 1}),
    )
    has_right, right = place + 1 < n_ctx, {"ctx": place + 1}
    has_left, left = place > 0, {"ctx": place - 1}
    has_next, following = section + 1 < n_section, {"section": section + 1}
    has_prev, previous = section > 0, {"section": section - 1}

    barrier = pltpu.get_barrier_semaphore()
    friends = around + ((has_right, right), (has_left, left), (has_next, following), (has_prev, previous))
    count = 0
    for there, device in friends:
        @pl.when(there)
        def _(device=device):
            pl.semaphore_signal(barrier, inc=1, device_id=device, device_id_type=MESH)
        count = count + there.astype(jnp.int32)
    pl.semaphore_wait(barrier, count)

    deep, half = wk_in.shape[0], wo_in.shape[0] // 2
    weights = (
        (wk_in, wk, False, 0, deep), (wv_in, wv, False, 0, deep), (wq_in, wq, False, 0, deep),
        (wo_in, wo, True, 0, half), (wo_in, wo, False, half, half),
    )
    n_part = len(weights)

    def part(a, shard):
        source, whole, _, first, rows = weights[a]
        start = shard * source.shape[0] + first
        return whole.at[pl.ds(pl.multiple_of(start, rows), rows), :]

    def shard_of(a):
        return weights[a][0].at[pl.ds(weights[a][3], weights[a][4]), :]

    def hop(a, shard, way, own):
        there, device = around[way]
        return there, pltpu.make_async_remote_copy(
            src_ref=shard_of(a) if own else part(a, shard),
            dst_ref=part(a, shard),
            send_sem=g_send.at[a, shard, way],
            recv_sem=g_recv.at[a, shard],
            device_id=device,
            device_id_type=MESH,
        )

    def ways_on(x_first, dz, dx):
        along_z = (0,) if dz > 0 else (1,)
        along_x = (2,) if dx > 0 else (3,)
        if x_first:
            return along_z if dz else along_x + (0, 1)
        return along_x if dx else along_z + (2, 3)

    offsets = [
        (dz, dx)
        for dz in range(1 - tall, tall)
        for dx in range(1 - wide, wide)
        if (dz, dx) != (0, 0)
    ]
    offsets.sort(key=lambda o: (abs(o[0]) + abs(o[1]), o))

    n_near = sum(abs(dz) + abs(dx) <= tall + wide - 4 for dz, dx in offsets)
    is_first = section % 2 == 0

    def gather(first):
        for a in range(n_part):
            for way in range(4):
                there, copy = hop(a, place, way, True)

                @pl.when(there)
                def _(copy=copy):
                    copy.start() if first else copy.wait_send()
        for spot, (dz, dx) in enumerate(offsets):
            if first and spot == n_near:
                @pl.when(is_first & has_next)
                def _():
                    pl.semaphore_signal(go_sem, inc=1, device_id=following, device_id_type=MESH)
            zs, xs = z - dz, x - dx
            inside = (zs >= 0) & (zs < tall) & (xs >= 0) & (xs < wide)

            @pl.when(inside)
            def _(dz=dz, dx=dx, shard=zs * wide + xs):
                for a in range(n_part):
                    if first:
                        hop(a, shard, 0, False)[1].wait_recv()
                    for way in ways_on(weights[a][2], dz, dx):
                        there, copy = hop(a, shard, way, False)

                        @pl.when(there)
                        def _(copy=copy):
                            copy.start() if first else copy.wait_send()

    own_copies = [
        pltpu.make_async_copy(shard_of(a), part(a, place), own_sem.at[a]) for a in range(n_part)
    ]
    x_copy = pltpu.make_async_copy(x0_ref, xbuf, in_sem.at[0])
    g_copy = pltpu.make_async_copy(cot_ref, gbuf, in_sem.at[1])
    for copy in own_copies:
        copy.start()

    @pl.when(section == 0)
    def _():
        x_copy.start()

    @pl.when(section == n_section - 1)
    def _():
        g_copy.start()

    kv[...] = jnp.zeros_like(kv)
    rims[...] = jnp.zeros_like(rims)

    @pl.when(jnp.logical_not(is_first))
    def _():
        pl.semaphore_wait(go_sem, 1)

    gather(True)
    for copy in own_copies:
        copy.wait()

    def relay(source, target, send, recv, device, c):
        cols = pl.ds(c * STEP, STEP)
        return pltpu.make_async_remote_copy(
            src_ref=source.at[:, cols], dst_ref=target.at[:, cols],
            send_sem=send.at[c], recv_sem=recv.at[c], device_id=device, device_id_type=MESH,
        )

    n_relay = D // STEP
    chunk = 64
    n_back = rows_all // chunk

    def relay_back(device, i):
        rows = pl.ds(pl.multiple_of(i * chunk, chunk), chunk)
        return pltpu.make_async_remote_copy(
            src_ref=grad_ref.at[rows, :], dst_ref=gbuf.at[rows, :],
            send_sem=b_send.at[i], recv_sem=b_recv.at[i], device_id=device, device_id_type=MESH,
        )

    @pl.when(section == 0)
    def _():
        x_copy.wait()

    @pl.when(has_prev)
    def _():
        gather(False)
        for c in range(n_relay):
            relay(out_ref, xbuf, x_send, x_recv, previous, c).wait_recv()

    @pl.loop(0, rows_all // chunk)
    def _(i):
        rows = pl.ds(pl.multiple_of(i * chunk, chunk), chunk)
        values = xbuf[rows, :].astype(F32)
        nbuf[rows, :] = (values * lax.rsqrt(head_mean(values * values) + EPS)).astype(BF16)

    def norm_heads(values):
        scales = []
        for h in range(STEP // HDIM):
            one = values[:, h * HDIM:(h + 1) * HDIM]
            scale = lax.rsqrt(head_mean(one * one) + EPS)
            scales.append(jnp.broadcast_to(scale, one.shape))
        return jnp.concatenate(scales, axis=1)

    @pl.loop(0, WIDTH // STEP)
    def _(i):
        cols = pl.ds(pl.multiple_of(i * STEP, STEP), STEP)
        out = dot(nbuf[...], wk[:, cols])
        scale = norm_heads(out)
        rk[:, cols] = scale
        key = (out * scale).astype(BF16)
        for m in range(micro):
            kv[0, m, BLK:BLK + length, cols] = key[m * length:(m + 1) * length]
        value = dot(nbuf[...], wv[:, cols]).astype(BF16)
        for m in range(micro):
            kv[1, m, BLK:BLK + length, cols] = value[m * length:(m + 1) * length]

    def to_right():
        return pltpu.make_async_remote_copy(
            src_ref=kv.at[:, :, pl.ds(length, BLK), :], dst_ref=kv.at[:, :, pl.ds(0, BLK), :],
            send_sem=h_send.at[0], recv_sem=h_recv.at[0], device_id=right, device_id_type=MESH,
        )

    def to_left():
        return pltpu.make_async_remote_copy(
            src_ref=kv.at[:, :, pl.ds(BLK, BLK), :], dst_ref=kv.at[:, :, pl.ds(BLK + length, BLK), :],
            send_sem=h_send.at[1], recv_sem=h_recv.at[1], device_id=left, device_id_type=MESH,
        )

    @pl.when(has_right)
    def _():
        to_right().start()

    @pl.when(has_left)
    def _():
        to_left().start()

    @pl.loop(0, WIDTH // STEP)
    def _(i):
        cols = pl.ds(pl.multiple_of(i * STEP, STEP), STEP)
        out = dot(nbuf[...], wq[:, cols])
        scale = norm_heads(out)
        rq[:, cols] = scale
        qbuf[:, cols] = (out * scale).astype(BF16)

    @pl.when(has_left)
    def _():
        to_right().wait_recv()

    @pl.when(has_right)
    def _():
        to_left().wait_recv()

    @pl.loop(0, HEADS, unroll=4)
    def _(h):
        cols = pl.ds(pl.multiple_of(h * HDIM, HDIM), HDIM)
        for m in range(micro):
            rows = slice(m * length, (m + 1) * length)
            scores = dot(qbuf[rows, cols], kv[0, m, :, cols], ((1,), (1,))) * HDIM ** (-0.5)
            prob = jnp.exp(scores) * mask_ref[m]
            probs[m, h] = prob
            inv = 1.0 / jnp.sum(prob, axis=-1, keepdims=True)
            inv_total[rows, cols] = jnp.broadcast_to(inv, (length, HDIM))
            att[rows, cols] = (dot(prob.astype(BF16), kv[1, m, :, cols]) * inv).astype(BF16)

    for c in range(n_relay):
        cols = slice(c * STEP, (c + 1) * STEP)
        update = dot(att[...], wo[:, cols])
        out_ref[:, cols] = (xbuf[:, cols].astype(F32) + update).astype(BF16)

        @pl.when(has_next)
        def _(c=c):
            relay(out_ref, xbuf, x_send, x_recv, following, c).start()

    @pl.when(section == 0)
    def _():
        gather(False)

    @pl.when(has_next)
    def _():
        for c in range(n_relay):
            relay(out_ref, xbuf, x_send, x_recv, following, c).wait_send()

    @pl.when(section == n_section - 1)
    def _():
        g_copy.wait()

    for m in range(micro):
        rows = slice(m * length, (m + 1) * length)

        @pl.when(has_next)
        def _(m=m):
            for i in range(m * length // chunk, (m + 1) * length // chunk):
                relay_back(following, i).wait_recv()

        @pl.loop(0, WIDTH // STEP)
        def _(i, rows=rows):
            cols = pl.ds(pl.multiple_of(i * STEP, STEP), STEP)
            datt[rows, cols] = dot(gbuf[rows, :], wo[cols, :], ((1,), (1,))).astype(BF16)

        @pl.loop(0, HEADS, unroll=4)
        def _(h, m=m, rows=rows):
            cols = pl.ds(pl.multiple_of(h * HDIM, HDIM), HDIM)
            prob = probs[m, h]
            d_att = datt[rows, cols].astype(F32)
            d_sum = d_att * inv_total[rows, cols]
            d_total = jnp.sum(d_sum * att[rows, cols].astype(F32), axis=-1, keepdims=True)
            d_sum = d_sum.astype(BF16)
            d_prob = dot(d_sum, kv[1, m, :, cols], ((1,), (1,))) - d_total
            d_score = (d_prob * prob * HDIM ** (-0.5)).astype(BF16)
            dkv[1, m, :, cols] = dot(prob.astype(BF16), d_sum, ((0,), (0,))).astype(BF16)
            dkv[0, m, :, cols] = dot(d_score, qbuf[rows, cols], ((0,), (0,))).astype(BF16)
            d_query = dot(d_score, kv[0, m, :, cols])
            query = qbuf[rows, cols].astype(F32)
            d_query = (d_query - query * head_mean(d_query * query)) * rq[rows, cols]
            dq[rows, cols] = d_query.astype(BF16)

    def rim_left():
        return pltpu.make_async_remote_copy(
            src_ref=dkv.at[:, :, pl.ds(0, BLK), :], dst_ref=rims.at[1],
            send_sem=r_send.at[0], recv_sem=r_recv.at[0], device_id=left, device_id_type=MESH,
        )

    def rim_right():
        return pltpu.make_async_remote_copy(
            src_ref=dkv.at[:, :, pl.ds(BLK + length, BLK), :], dst_ref=rims.at[0],
            send_sem=r_send.at[1], recv_sem=r_recv.at[1], device_id=right, device_id_type=MESH,
        )

    @pl.when(has_left)
    def _():
        rim_left().start()

    @pl.when(has_right)
    def _():
        rim_right().start()

    @pl.loop(0, D // STEP)
    def _(i):
        cols = pl.ds(pl.multiple_of(i * STEP, STEP), STEP)
        dn[:, cols] = dot(dq[...], wq[cols, :], ((1,), (1,)))

    @pl.when(has_right)
    def _():
        rim_left().wait_recv()

    @pl.when(has_left)
    def _():
        rim_right().wait_recv()

    for which in range(2):
        for m in range(micro):
            for side, start in ((0, BLK), (1, length)):
                rows = slice(start, start + BLK)
                dkv[which, m, rows] = dkv[which, m, rows] + rims[side, which, m]

    @pl.loop(0, HEADS, unroll=4)
    def _(h):
        cols = pl.ds(pl.multiple_of(h * HDIM, HDIM), HDIM)
        for m in range(micro):
            rows = slice(m * length, (m + 1) * length)
            d_key = dkv[0, m, BLK:BLK + length, cols].astype(F32)
            key = kv[0, m, BLK:BLK + length, cols].astype(F32)
            d_key = (d_key - key * head_mean(d_key * key)) * rk[rows, cols]
            dq[rows, cols] = d_key.astype(BF16)
            datt[rows, cols] = dkv[1, m, BLK:BLK + length, cols]

    @pl.loop(0, D // STEP)
    def _(i):
        cols = pl.ds(pl.multiple_of(i * STEP, STEP), STEP)
        dn[:, cols] = (
            dn[:, cols]
            + dot(dq[...], wk[cols, :], ((1,), (1,)))
            + dot(datt[...], wv[cols, :], ((1,), (1,)))
        )

    @pl.loop(0, rows_all // chunk)
    def _(i):
        rows = pl.ds(pl.multiple_of(i * chunk, chunk), chunk)
        values = xbuf[rows, :].astype(F32)
        scale = lax.rsqrt(head_mean(values * values) + EPS)
        d_norm = dn[rows, :].astype(BF16).astype(F32)
        normed = values * scale
        d_in = scale * (d_norm - normed * head_mean(d_norm * normed))
        grad_ref[rows, :] = (gbuf[rows, :].astype(F32) + d_in.astype(BF16).astype(F32)).astype(BF16)

        @pl.when(has_prev)
        def _():
            relay_back(previous, i).start()

    @pl.when(has_right)
    def _():
        to_right().wait_send()
        rim_right().wait_send()

    @pl.when(has_left)
    def _():
        to_left().wait_send()
        rim_left().wait_send()

    @pl.when(has_prev)
    def _():
        for i in range(n_back):
            relay_back(previous, i).wait_send()


def mask_weights(block_mask, place, n_ctx, length):
    blocks = length // BLK
    ids = place * blocks + jnp.arange(blocks)
    mask = block_mask.astype(F32)
    before = mask[:, :, 0] * (ids > 0).astype(F32)
    after = mask[:, :, 1] * (ids < blocks * n_ctx - 1).astype(F32)
    offset = jnp.arange(EXT)[None, :] // BLK - jnp.arange(length)[:, None] // BLK
    def rows(values):
        return jnp.repeat(values, BLK, axis=1)[:, :, None]
    return jnp.where(offset == 0, rows(before), jnp.where(offset == 1, 1.0, jnp.where(offset == 2, rows(after), 0.0)))


def per_device(n_section, n_ctx, section_input, cotangent, w_query, w_key, w_value, w_out, block_mask):
    micro, length = section_input.shape[:2]
    rows = micro * length
    mask = mask_weights(block_mask, lax.axis_index("ctx"), n_ctx, length)
    any_space = pl.BlockSpec(memory_space=pl.ANY)
    vmem = pl.BlockSpec(memory_space=pltpu.VMEM)
    dma = pltpu.SemaphoreType.DMA
    n_relay = D // STEP
    out, grad = pl.pallas_call(
        functools.partial(kernel, n_section, n_ctx, micro, length),
        out_shape=[jax.ShapeDtypeStruct((rows, D), BF16)] * 2,
        in_specs=[any_space] * 6 + [vmem],
        out_specs=[vmem, vmem],
        scratch_shapes=[
            pltpu.VMEM((D, WIDTH), BF16),
            pltpu.VMEM((D, WIDTH), BF16),
            pltpu.VMEM((D, WIDTH), BF16),
            pltpu.VMEM((WIDTH, D), BF16),
            pltpu.VMEM((rows, D), BF16),
            pltpu.VMEM((rows, D), BF16),
            pltpu.VMEM((rows, D), BF16),
            pltpu.VMEM((rows, WIDTH), BF16),
            pltpu.VMEM((rows, WIDTH), F32),
            pltpu.VMEM((rows, WIDTH), F32),
            pltpu.VMEM((2, micro, EXT, WIDTH), BF16),
            pltpu.VMEM((rows, WIDTH), BF16),
            pltpu.VMEM((rows, WIDTH), F32),
            pltpu.VMEM((micro, HEADS, length, EXT), F32),
            pltpu.VMEM((rows, WIDTH), BF16),
            pltpu.VMEM((rows, WIDTH), BF16),
            pltpu.VMEM((2, micro, EXT, WIDTH), BF16),
            pltpu.VMEM((2, 2, micro, BLK, WIDTH), BF16),
            pltpu.VMEM((rows, D), F32),
            dma((5, n_ctx)),
            dma((5, n_ctx, 4)),
            dma((5,)),
            dma((n_relay,)),
            dma((n_relay,)),
            dma((rows // 64,)),
            dma((rows // 64,)),
            dma((2,)),
            dma((2,)),
            dma((2,)),
            dma((2,)),
            dma((2,)),
            pltpu.SemaphoreType.REGULAR,
        ],
        compiler_params=pltpu.CompilerParams(
            collective_id=0, has_side_effects=True, vmem_limit_bytes=56 * 2**20
        ),
    )(
        section_input.reshape(rows, D), cotangent.reshape(rows, D),
        w_query[0], w_key[0], w_value[0], w_out[0], mask,
    )
    return out.reshape(1, micro, length, D), grad.reshape(1, micro, length, D)


def solution(mesh):
    return jax.shard_map(
        functools.partial(per_device, mesh.shape["section"], mesh.shape["ctx"]),
        mesh=mesh,
        in_specs=(
            P(None, "ctx", None),
            P(None, "ctx", None),
            P("section", "ctx", None),
            P("section", "ctx", None),
            P("section", "ctx", None),
            P("section", "ctx", None),
            P(None, "ctx", None),
        ),
        out_specs=(P("section", None, "ctx", None), P("section", None, "ctx", None)),
        check_vma=False,
    )
```

```python
import functools

import jax
import jax.numpy as jnp
from jax import lax
from jax.experimental import pallas as pl
from jax.experimental.pallas import tpu as pltpu
from jax.sharding import PartitionSpec as P

D = 2048
HEADS = 8
HDIM = 128
WIDTH = HEADS * HDIM
BLK = 32
EPS = 1e-06
EXT = 256
STEP = 512
MESH = pl.DeviceIdType.MESH
F32 = jnp.float32
BF16 = jnp.bfloat16


def grid_of(n_ctx):
    wide = 1
    while (2 * wide) * (2 * wide) * 2 <= n_ctx:
        wide *= 2
    return n_ctx // wide, wide


def dot(a, b, dims=((1,), (0,))):
    return lax.dot_general(a, b, (dims, ((), ())), preferred_element_type=F32)


def head_mean(values):
    return jnp.mean(values, axis=-1, keepdims=True)


def kernel(
    n_section, n_ctx, micro, length,
    x0_ref, cot_ref, wq_in, wk_in, wv_in, wo_in, mask_ref,
    out_ref, grad_ref,
    wq, wk, wv, wo, wq_t, wk_t, wv_t, wo_t, xbuf, gbuf, nbuf, qbuf, rq, rk, kv, att, inv_total, probs,
    datt, dq, dkv, rims, dn,
    g_recv, g_send, own_sem, x_recv, x_send, b_recv, b_send, h_recv, h_send, r_recv, r_send, in_sem, go_sem,
):
    section = lax.axis_index("section")
    place = lax.axis_index("ctx")
    tall, wide = grid_of(n_ctx)
    z = place // wide
    x = place % wide
    rows_all = micro * length

    around = (
        (z + 1 < tall, {"ctx": place + wide}),
        (z > 0, {"ctx": place - wide}),
        (x + 1 < wide, {"ctx": place + 1}),
        (x > 0, {"ctx": place - 1}),
    )
    has_right, right = place + 1 < n_ctx, {"ctx": place + 1}
    has_left, left = place > 0, {"ctx": place - 1}
    has_next, following = section + 1 < n_section, {"section": section + 1}
    has_prev, previous = section > 0, {"section": section - 1}

    barrier = pltpu.get_barrier_semaphore()
    friends = around + ((has_right, right), (has_left, left), (has_next, following), (has_prev, previous))
    count = 0
    for there, device in friends:
        @pl.when(there)
        def _(device=device):
            pl.semaphore_signal(barrier, inc=1, device_id=device, device_id_type=MESH)
        count = count + there.astype(jnp.int32)
    pl.semaphore_wait(barrier, count)

    deep, half = wk_in.shape[0], wo_in.shape[0] // 2
    weights = (
        (wk_in, wk, False, 0, deep), (wv_in, wv, False, 0, deep), (wq_in, wq, False, 0, deep),
        (wo_in, wo, True, 0, half), (wo_in, wo, False, half, half),
    )
    n_part = len(weights)

    def part(a, shard):
        source, whole, _, first, rows = weights[a]
        start = shard * source.shape[0] + first
        return whole.at[pl.ds(pl.multiple_of(start, rows), rows), :]

    def shard_of(a):
        return weights[a][0].at[pl.ds(weights[a][3], weights[a][4]), :]

    def hop(a, shard, way, own):
        there, device = around[way]
        return there, pltpu.make_async_remote_copy(
            src_ref=shard_of(a) if own else part(a, shard),
            dst_ref=part(a, shard),
            send_sem=g_send.at[a, shard, way],
            recv_sem=g_recv.at[a, shard],
            device_id=device,
            device_id_type=MESH,
        )

    def ways_on(x_first, dz, dx):
        along_z = (0,) if dz > 0 else (1,)
        along_x = (2,) if dx > 0 else (3,)
        if x_first:
            return along_z if dz else along_x + (0, 1)
        return along_x if dx else along_z + (2, 3)

    offsets = [
        (dz, dx)
        for dz in range(1 - tall, tall)
        for dx in range(1 - wide, wide)
        if (dz, dx) != (0, 0)
    ]
    offsets.sort(key=lambda o: (abs(o[0]) + abs(o[1]), o))

    n_near = sum(abs(dz) + abs(dx) <= tall + wide - 4 for dz, dx in offsets)
    is_first = section % 2 == 0

    def gather(first):
        for a in range(n_part):
            for way in range(4):
                there, copy = hop(a, place, way, True)

                @pl.when(there)
                def _(copy=copy):
                    copy.start() if first else copy.wait_send()
        for spot, (dz, dx) in enumerate(offsets):
            if first and spot == n_near:
                @pl.when(is_first & has_next)
                def _():
                    pl.semaphore_signal(go_sem, inc=1, device_id=following, device_id_type=MESH)
            zs, xs = z - dz, x - dx
            inside = (zs >= 0) & (zs < tall) & (xs >= 0) & (xs < wide)

            @pl.when(inside)
            def _(dz=dz, dx=dx, shard=zs * wide + xs):
                for a in range(n_part):
                    if first:
                        hop(a, shard, 0, False)[1].wait_recv()
                    for way in ways_on(weights[a][2], dz, dx):
                        there, copy = hop(a, shard, way, False)

                        @pl.when(there)
                        def _(copy=copy):
                            copy.start() if first else copy.wait_send()

    own_copies = [
        pltpu.make_async_copy(shard_of(a), part(a, place), own_sem.at[a]) for a in range(n_part)
    ]
    x_copy = pltpu.make_async_copy(x0_ref, xbuf, in_sem.at[0])
    g_copy = pltpu.make_async_copy(cot_ref, gbuf, in_sem.at[1])
    for copy in own_copies:
        copy.start()

    @pl.when(section == 0)
    def _():
        x_copy.start()

    @pl.when(section == n_section - 1)
    def _():
        g_copy.start()

    kv[...] = jnp.zeros_like(kv)
    rims[...] = jnp.zeros_like(rims)

    @pl.when(jnp.logical_not(is_first))
    def _():
        pl.semaphore_wait(go_sem, 1)

    gather(True)
    for copy in own_copies:
        copy.wait()

    def relay(source, target, send, recv, device, c):
        cols = pl.ds(c * STEP, STEP)
        return pltpu.make_async_remote_copy(
            src_ref=source.at[:, cols], dst_ref=target.at[:, cols],
            send_sem=send.at[c], recv_sem=recv.at[c], device_id=device, device_id_type=MESH,
        )

    n_relay = D // STEP
    chunk = 64
    n_back = rows_all // chunk

    def relay_back(device, i):
        rows = pl.ds(pl.multiple_of(i * chunk, chunk), chunk)
        return pltpu.make_async_remote_copy(
            src_ref=grad_ref.at[rows, :], dst_ref=gbuf.at[rows, :],
            send_sem=b_send.at[i], recv_sem=b_recv.at[i], device_id=device, device_id_type=MESH,
        )

    @pl.when(section == 0)
    def _():
        x_copy.wait()

    def turn():
        @pl.loop(0, D // EXT)
        def _(i):
            rows = pl.ds(pl.multiple_of(i * EXT, EXT), EXT)
            for whole, turned in ((wq, wq_t), (wk, wk_t), (wv, wv_t)):
                turned[:, rows] = whole[rows, :].T

        @pl.loop(0, WIDTH // EXT)
        def _(i):
            rows = pl.ds(pl.multiple_of(i * EXT, EXT), EXT)
            wo_t[:, rows] = wo[rows, :].T

    @pl.when(section >= 2)
    def _():
        turn()

    @pl.when(has_prev)
    def _():
        gather(False)
        for c in range(n_relay):
            relay(out_ref, xbuf, x_send, x_recv, previous, c).wait_recv()

    @pl.loop(0, rows_all // chunk)
    def _(i):
        rows = pl.ds(pl.multiple_of(i * chunk, chunk), chunk)
        values = xbuf[rows, :].astype(F32)
        nbuf[rows, :] = (values * lax.rsqrt(head_mean(values * values) + EPS)).astype(BF16)

    def norm_heads(values):
        scales = []
        for h in range(STEP // HDIM):
            one = values[:, h * HDIM:(h + 1) * HDIM]
            scale = lax.rsqrt(head_mean(one * one) + EPS)
            scales.append(jnp.broadcast_to(scale, one.shape))
        return jnp.concatenate(scales, axis=1)

    @pl.loop(0, WIDTH // STEP)
    def _(i):
        cols = pl.ds(pl.multiple_of(i * STEP, STEP), STEP)
        out = dot(nbuf[...], wk[:, cols])
        scale = norm_heads(out)
        rk[:, cols] = scale
        key = (out * scale).astype(BF16)
        for m in range(micro):
            kv[0, m, BLK:BLK + length, cols] = key[m * length:(m + 1) * length]
        value = dot(nbuf[...], wv[:, cols]).astype(BF16)
        for m in range(micro):
            kv[1, m, BLK:BLK + length, cols] = value[m * length:(m + 1) * length]

    def to_right():
        return pltpu.make_async_remote_copy(
            src_ref=kv.at[:, :, pl.ds(length, BLK), :], dst_ref=kv.at[:, :, pl.ds(0, BLK), :],
            send_sem=h_send.at[0], recv_sem=h_recv.at[0], device_id=right, device_id_type=MESH,
        )

    def to_left():
        return pltpu.make_async_remote_copy(
            src_ref=kv.at[:, :, pl.ds(BLK, BLK), :], dst_ref=kv.at[:, :, pl.ds(BLK + length, BLK), :],
            send_sem=h_send.at[1], recv_sem=h_recv.at[1], device_id=left, device_id_type=MESH,
        )

    @pl.when(has_right)
    def _():
        to_right().start()

    @pl.when(has_left)
    def _():
        to_left().start()

    @pl.loop(0, WIDTH // STEP)
    def _(i):
        cols = pl.ds(pl.multiple_of(i * STEP, STEP), STEP)
        out = dot(nbuf[...], wq[:, cols])
        scale = norm_heads(out)
        rq[:, cols] = scale
        qbuf[:, cols] = (out * scale).astype(BF16)

    @pl.when(has_left)
    def _():
        to_right().wait_recv()

    @pl.when(has_right)
    def _():
        to_left().wait_recv()

    @pl.loop(0, HEADS, unroll=4)
    def _(h):
        cols = pl.ds(pl.multiple_of(h * HDIM, HDIM), HDIM)
        for m in range(micro):
            rows = slice(m * length, (m + 1) * length)
            scores = dot(qbuf[rows, cols], kv[0, m, :, cols], ((1,), (1,))) * HDIM ** (-0.5)
            prob = jnp.exp(scores) * mask_ref[m]
            probs[m, h] = prob
            inv = 1.0 / jnp.sum(prob, axis=-1, keepdims=True)
            inv_total[rows, cols] = jnp.broadcast_to(inv, (length, HDIM))
            att[rows, cols] = (dot(prob.astype(BF16), kv[1, m, :, cols]) * inv).astype(BF16)

    for c in range(n_relay):
        cols = slice(c * STEP, (c + 1) * STEP)
        update = dot(att[...], wo[:, cols])
        out_ref[:, cols] = (xbuf[:, cols].astype(F32) + update).astype(BF16)

        @pl.when(has_next)
        def _(c=c):
            relay(out_ref, xbuf, x_send, x_recv, following, c).start()

    @pl.when(section < 2)
    def _():
        turn()

    @pl.when(section == 0)
    def _():
        gather(False)

    @pl.when(has_next)
    def _():
        for c in range(n_relay):
            relay(out_ref, xbuf, x_send, x_recv, following, c).wait_send()

    @pl.when(section == n_section - 1)
    def _():
        g_copy.wait()

    for m in range(micro):
        rows = slice(m * length, (m + 1) * length)

        @pl.when(has_next)
        def _(m=m):
            for i in range(m * length // chunk, (m + 1) * length // chunk):
                relay_back(following, i).wait_recv()

        @pl.loop(0, WIDTH // STEP)
        def _(i, rows=rows):
            cols = pl.ds(pl.multiple_of(i * STEP, STEP), STEP)
            datt[rows, cols] = dot(gbuf[rows, :], wo_t[:, cols]).astype(BF16)

        @pl.loop(0, HEADS, unroll=4)
        def _(h, m=m, rows=rows):
            cols = pl.ds(pl.multiple_of(h * HDIM, HDIM), HDIM)
            prob = probs[m, h]
            d_att = datt[rows, cols].astype(F32)
            d_sum = d_att * inv_total[rows, cols]
            d_total = jnp.sum(d_sum * att[rows, cols].astype(F32), axis=-1, keepdims=True)
            d_sum = d_sum.astype(BF16)
            d_prob = dot(d_sum, kv[1, m, :, cols], ((1,), (1,))) - d_total
            d_score = (d_prob * prob * HDIM ** (-0.5)).astype(BF16)
            dkv[1, m, :, cols] = dot(prob.astype(BF16), d_sum, ((0,), (0,))).astype(BF16)
            dkv[0, m, :, cols] = dot(d_score, qbuf[rows, cols], ((0,), (0,))).astype(BF16)
            d_query = dot(d_score, kv[0, m, :, cols])
            query = qbuf[rows, cols].astype(F32)
            d_query = (d_query - query * head_mean(d_query * query)) * rq[rows, cols]
            dq[rows, cols] = d_query.astype(BF16)

    def rim_left():
        return pltpu.make_async_remote_copy(
            src_ref=dkv.at[:, :, pl.ds(0, BLK), :], dst_ref=rims.at[1],
            send_sem=r_send.at[0], recv_sem=r_recv.at[0], device_id=left, device_id_type=MESH,
        )

    def rim_right():
        return pltpu.make_async_remote_copy(
            src_ref=dkv.at[:, :, pl.ds(BLK + length, BLK), :], dst_ref=rims.at[0],
            send_sem=r_send.at[1], recv_sem=r_recv.at[1], device_id=right, device_id_type=MESH,
        )

    @pl.when(has_left)
    def _():
        rim_left().start()

    @pl.when(has_right)
    def _():
        rim_right().start()

    @pl.loop(0, D // STEP)
    def _(i):
        cols = pl.ds(pl.multiple_of(i * STEP, STEP), STEP)
        dn[:, cols] = dot(dq[...], wq_t[:, cols])

    @pl.when(has_right)
    def _():
        rim_left().wait_recv()

    @pl.when(has_left)
    def _():
        rim_right().wait_recv()

    for which in range(2):
        for m in range(micro):
            for side, start in ((0, BLK), (1, length)):
                rows = slice(start, start + BLK)
                dkv[which, m, rows] = dkv[which, m, rows] + rims[side, which, m]

    @pl.loop(0, HEADS, unroll=4)
    def _(h):
        cols = pl.ds(pl.multiple_of(h * HDIM, HDIM), HDIM)
        for m in range(micro):
            rows = slice(m * length, (m + 1) * length)
            d_key = dkv[0, m, BLK:BLK + length, cols].astype(F32)
            key = kv[0, m, BLK:BLK + length, cols].astype(F32)
            d_key = (d_key - key * head_mean(d_key * key)) * rk[rows, cols]
            dq[rows, cols] = d_key.astype(BF16)
            datt[rows, cols] = dkv[1, m, BLK:BLK + length, cols]

    @pl.loop(0, D // STEP)
    def _(i):
        cols = pl.ds(pl.multiple_of(i * STEP, STEP), STEP)
        dn[:, cols] = (
            dn[:, cols]
            + dot(dq[...], wk_t[:, cols])
            + dot(datt[...], wv_t[:, cols])
        )

    @pl.loop(0, rows_all // chunk)
    def _(i):
        rows = pl.ds(pl.multiple_of(i * chunk, chunk), chunk)
        values = xbuf[rows, :].astype(F32)
        scale = lax.rsqrt(head_mean(values * values) + EPS)
        d_norm = dn[rows, :].astype(BF16).astype(F32)
        normed = values * scale
        d_in = scale * (d_norm - normed * head_mean(d_norm * normed))
        grad_ref[rows, :] = (gbuf[rows, :].astype(F32) + d_in.astype(BF16).astype(F32)).astype(BF16)

        @pl.when(has_prev)
        def _():
            relay_back(previous, i).start()

    @pl.when(has_right)
    def _():
        to_right().wait_send()
        rim_right().wait_send()

    @pl.when(has_left)
    def _():
        to_left().wait_send()
        rim_left().wait_send()

    @pl.when(has_prev)
    def _():
        for i in range(n_back):
            relay_back(previous, i).wait_send()


def mask_weights(block_mask, place, n_ctx, length):
    blocks = length // BLK
    ids = place * blocks + jnp.arange(blocks)
    mask = block_mask.astype(F32)
    before = mask[:, :, 0] * (ids > 0).astype(F32)
    after = mask[:, :, 1] * (ids < blocks * n_ctx - 1).astype(F32)
    offset = jnp.arange(EXT)[None, :] // BLK - jnp.arange(length)[:, None] // BLK
    def rows(values):
        return jnp.repeat(values, BLK, axis=1)[:, :, None]
    return jnp.where(offset == 0, rows(before), jnp.where(offset == 1, 1.0, jnp.where(offset == 2, rows(after), 0.0)))


def per_device(n_section, n_ctx, section_input, cotangent, w_query, w_key, w_value, w_out, block_mask):
    micro, length = section_input.shape[:2]
    rows = micro * length
    mask = mask_weights(block_mask, lax.axis_index("ctx"), n_ctx, length)
    any_space = pl.BlockSpec(memory_space=pl.ANY)
    vmem = pl.BlockSpec(memory_space=pltpu.VMEM)
    dma = pltpu.SemaphoreType.DMA
    n_relay = D // STEP
    out, grad = pl.pallas_call(
        functools.partial(kernel, n_section, n_ctx, micro, length),
        out_shape=[jax.ShapeDtypeStruct((rows, D), BF16)] * 2,
        in_specs=[any_space] * 6 + [vmem],
        out_specs=[vmem, vmem],
        scratch_shapes=[
            pltpu.VMEM((D, WIDTH), BF16),
            pltpu.VMEM((D, WIDTH), BF16),
            pltpu.VMEM((D, WIDTH), BF16),
            pltpu.VMEM((WIDTH, D), BF16),
            pltpu.VMEM((WIDTH, D), BF16),
            pltpu.VMEM((WIDTH, D), BF16),
            pltpu.VMEM((WIDTH, D), BF16),
            pltpu.VMEM((D, WIDTH), BF16),
            pltpu.VMEM((rows, D), BF16),
            pltpu.VMEM((rows, D), BF16),
            pltpu.VMEM((rows, D), BF16),
            pltpu.VMEM((rows, WIDTH), BF16),
            pltpu.VMEM((rows, WIDTH), F32),
            pltpu.VMEM((rows, WIDTH), F32),
            pltpu.VMEM((2, micro, EXT, WIDTH), BF16),
            pltpu.VMEM((rows, WIDTH), BF16),
            pltpu.VMEM((rows, WIDTH), F32),
            pltpu.VMEM((micro, HEADS, length, EXT), F32),
            pltpu.VMEM((rows, WIDTH), BF16),
            pltpu.VMEM((rows, WIDTH), BF16),
            pltpu.VMEM((2, micro, EXT, WIDTH), BF16),
            pltpu.VMEM((2, 2, micro, BLK, WIDTH), BF16),
            pltpu.VMEM((rows, D), F32),
            dma((5, n_ctx)),
            dma((5, n_ctx, 4)),
            dma((5,)),
            dma((n_relay,)),
            dma((n_relay,)),
            dma((rows // 64,)),
            dma((rows // 64,)),
            dma((2,)),
            dma((2,)),
            dma((2,)),
            dma((2,)),
            dma((2,)),
            pltpu.SemaphoreType.REGULAR,
        ],
        compiler_params=pltpu.CompilerParams(
            collective_id=0, has_side_effects=True, vmem_limit_bytes=60 * 2**20
        ),
    )(
        section_input.reshape(rows, D), cotangent.reshape(rows, D),
        w_query[0], w_key[0], w_value[0], w_out[0], mask,
    )
    return out.reshape(1, micro, length, D), grad.reshape(1, micro, length, D)


def solution(mesh):
    return jax.shard_map(
        functools.partial(per_device, mesh.shape["section"], mesh.shape["ctx"]),
        mesh=mesh,
        in_specs=(
            P(None, "ctx", None),
            P(None, "ctx", None),
            P("section", "ctx", None),
            P("section", "ctx", None),
            P("section", "ctx", None),
            P("section", "ctx", None),
            P(None, "ctx", None),
        ),
        out_specs=(P("section", None, "ctx", None), P("section", None, "ctx", None)),
        check_vma=False,
    )
```
